32 devices in a mesh: section: 16 (over z, x, core), tensor: 2 (over y).
Axes of the slice: x: 2, y: 2, z: 4, core: 2. Of those that a mesh axis runs over, the one named last changes fastest.
Arguments:
- section_rows: bfloat16 [3, 2048, 8192], P(None, 'section', 'tensor'), may hold values from -6 to 6
- student_rows: bfloat16 [3, 2048, 3584], P(None, 'section'), may hold values from -6 to 6
- proj: bfloat16 [3584, 8192], P('section', 'tensor'), may hold values from -0.09375 to 0.09375
- gains: float32 [3, 8192], P(None, 'tensor'), may hold values from 0.1 to 1.9
- offsets: int32 [16], replicated, may hold values from 0 to 15, each once
Outputs:
- loss: float32 [], replicated
- grad_student: float32 [3, 2048, 3584], P(None, 'section', 'tensor')
- grad_proj: float32 [3584, 8192], P('section', 'tensor')
- grad_gains: float32 [3, 8192], P(None, 'tensor')
The draws below stay inside these ranges and needn't reach their ends.
Inputs may be any that keep to these rules, and one draw needn't show every extreme that they name: `offsets`: each shard is held by exactly one rank.
All inputs are finite; a program needn't handle non-finite values.
Results may differ from the reference program's by a relative error of at most 0.01.
Values may be sent and summed in bfloat16 or wider, within the bound.
A program may use at most 192 MiB of HBM per device.

```python
import jax
import jax.numpy as jnp
from jax import lax

DT = 8192
DS = 3584
SEQ_DEV = 128
SEQ = 2048
N_SECTION = 16


def block_levels(key, extent, shards, least, high):
    gain, own = 1.0, jax.random.fold_in(key, 6)
    for dim, blocks in shards:
        heights = jnp.exp(jax.random.uniform(jax.random.fold_in(own, dim), (blocks,), jnp.float32, least / len(shards), high / len(shards)))
        gain = gain * jnp.repeat(heights, extent[dim] // blocks).reshape([-1 if axis == dim else 1 for axis in range(len(extent))])
    return gain


def centred(key, shape, deviation, most, shards=(), held_as=jnp.bfloat16):
    factor_of = block_levels(key, shape, shards, -0.22, 0.18) if shards else 1.0
    result = jax.random.normal(key, shape, jnp.float32) * deviation * factor_of
    return jnp.minimum(jnp.maximum(result, -most), most).astype(held_as)


def setup_inputs(seed: int = 0) -> dict:
    keys = jax.random.split(jax.random.key(seed), 6)
    return {
        "section_rows": centred(keys[0], (3, SEQ, DT), 1.0, 6.0, ((1, 16), (2, 2))),
        "student_rows": centred(keys[1], (3, SEQ, DS), 1.0, 6.0, ((1, 16),)),
        "proj": centred(keys[2], (DS, DT), DS ** -0.5, 0.09375, ((0, 16), (1, 2))),
        "gains": jnp.clip(1.0 + 0.18 * jax.random.normal(keys[3], (3, DT), jnp.float32), 0.1, 1.9),
        "offsets": jax.random.permutation(keys[4], N_SECTION).astype(jnp.int32),
    }


def reference(section_rows, student_rows, proj, gains, offsets):
    rescale = (3.0 * SEQ) ** -0.5
    natural = section_rows.reshape(3, N_SECTION, SEQ_DEV, DT).transpose(0, 2, 1, 3).reshape(3, SEQ, DT)
    target = jnp.take(natural.reshape(3, N_SECTION, SEQ_DEV, DT), offsets, axis=1).reshape(3, SEQ, DT).astype(jnp.float32)
    pred = jnp.stack([jnp.dot(student_rows[depth], proj, preferred_element_type=jnp.float32) for depth in range(3)])
    scale = jnp.mean(target * target, axis=-1, keepdims=True) + 1e-6
    diff = gains[:, None, :] * pred - target
    ratio = diff / scale
    loss = jnp.sum(diff * ratio) / (2.0 * 3 * SEQ * DT)
    steer = (gains[:, None, :] * ratio).astype(jnp.bfloat16)
    grad_student = jnp.stack([lax.dot_general(steer[depth], proj, (((1,), (1,)), ((), ())), preferred_element_type=jnp.float32) for depth in range(3)])
    grad_gains = jnp.sum(ratio * pred, axis=1) * rescale

    def add_shard(index, total):
        rows_student = lax.dynamic_slice_in_dim(student_rows, index * SEQ_DEV, SEQ_DEV, 1).reshape(3 * SEQ_DEV, DS)
        rows_steer = lax.dynamic_slice_in_dim(steer, index * SEQ_DEV, SEQ_DEV, 1).reshape(3 * SEQ_DEV, DT)
        term = lax.dot_general(rows_student, rows_steer, (((0,), (0,)), ((), ())), preferred_element_type=jnp.float32)
        rounded = lax.optimization_barrier(term.astype(jnp.bfloat16))
        return total + rounded.astype(jnp.float32)

    grad_proj = lax.fori_loop(0, N_SECTION, add_shard, jnp.zeros((DS, DT), jnp.float32)) * rescale
    return loss, grad_student, grad_proj, grad_gains
```

```python
import functools

import jax
import jax.numpy as jnp
from jax import lax
from jax.experimental import pallas as pl
from jax.experimental.pallas import tpu as pltpu
from jax.sharding import PartitionSpec as P

MESH = pl.DeviceIdType.MESH
SUBS = 2


def ring_place(index, n):
    chip, core = index // 2, index % 2
    if n == 16:
        z, x = chip // 2, chip % 2
        place = z + x * (7 - 2 * z)
    else:
        a, b = chip // 4, chip % 4
        place = a * 4 + b + (a % 2) * (3 - 2 * b)
    return place * 2 + core


def ring_index(place, n):
    spot, core = place // 2, place % 2
    if n == 16:
        x = spot // 4
        z = spot + x * (7 - 2 * spot)
        chip = z * 2 + x
    else:
        a, b = spot // 4, spot % 4
        chip = a * 4 + b + (a % 2) * (3 - 2 * b)
    return chip * 2 + core


def reduce_kernel(n, rescale, st_ref, steer_ref, out_ref, slots, send_sem, recv_sem):
    tensor = lax.axis_index("tensor")
    me = ring_place(lax.axis_index("section"), n)
    right = ring_index((me + 1) % n, n)
    left = ring_index((me + n - 1) % n, n)
    towards = (right, left)
    wide = slots.shape[-1]

    barrier = pltpu.get_barrier_semaphore()
    for neighbour in towards:
        pl.semaphore_signal(barrier, inc=1, device_id=(neighbour, tensor), device_id_type=MESH)
    pl.semaphore_wait(barrier, 2)

    def columns(d, j):
        return pl.ds((d * SUBS + j) * wide, wide)

    def term(d, j, step):
        place = (me + 2 * n - 1 - step) % n if d == 0 else (me + 1 + step) % n
        return jnp.dot(
            st_ref[ring_index(place, n)],
            steer_ref[:, columns(d, j)],
            preferred_element_type=jnp.float32,
        )

    def copy(d, j, step):
        return pltpu.make_async_remote_copy(
            src_ref=slots.at[d, j, step],
            dst_ref=slots.at[d, j, step + 1],
            send_sem=send_sem.at[d, j, step],
            recv_sem=recv_sem.at[d, j, step],
            device_id=(towards[d], tensor),
            device_id_type=MESH,
        )

    for j in range(SUBS):
        for d in range(2):
            slots[d, j, 0] = term(d, j, 0).astype(jnp.bfloat16)
            copy(d, j, 0).start()

    def body(step, carry):
        for j in range(SUBS):
            for d in range(2):
                own = term(d, j, step)
                copy(d, j, step - 1).wait_recv()
                slots[d, j, step] = (slots[d, j, step].astype(jnp.float32) + own).astype(
                    jnp.bfloat16
                )
                copy(d, j, step).start()
        return carry

    lax.fori_loop(1, n - 1, body, 0)
    for j in range(SUBS):
        for d in range(2):
            own = term(d, j, n - 1)
            copy(d, j, n - 2).wait_recv()
            out_ref[:, columns(d, j)] = (
                slots[d, j, n - 1].astype(jnp.float32) + own
            ) * rescale

    def drain(step, carry):
        for j in range(SUBS):
            for d in range(2):
                copy(d, j, step).wait_send()
        return carry

    lax.fori_loop(0, n - 1, drain, 0)


def reduce_terms(student_blocks, steer, n, rescale):
    rows = student_blocks.shape[1]
    width = steer.shape[1]
    wide = width // (2 * SUBS)
    return pl.pallas_call(
        functools.partial(reduce_kernel, n, rescale),
        out_shape=jax.ShapeDtypeStruct((rows, width), jnp.float32),
        in_specs=[pl.BlockSpec(memory_space=pltpu.VMEM)] * 2,
        out_specs=pl.BlockSpec(memory_space=pltpu.VMEM),
        scratch_shapes=[
            pltpu.VMEM((2, SUBS, n, rows, wide), jnp.bfloat16),
            pltpu.SemaphoreType.DMA((2, SUBS, n)),
            pltpu.SemaphoreType.DMA((2, SUBS, n)),
        ],
        compiler_params=pltpu.CompilerParams(
            collective_id=0, has_side_effects=True, vmem_limit_bytes=52 * 1024 * 1024
        ),
        cost_estimate=pl.CostEstimate(
            flops=2 * n * rows * width * steer.shape[0],
            bytes_accessed=400_000_000,
            transcendentals=0,
        ),
        name="reduce_terms",
    )(student_blocks, steer)


def body(section_rows, student_rows, proj, gains, offsets):
    sections = lax.axis_size("section")
    tensors = lax.axis_size("tensor")
    seq_dev = student_rows.shape[1]
    width = section_rows.shape[2]
    student_width = student_rows.shape[2]
    per_source = seq_dev // sections
    total_rows = 3 * seq_dev * sections
    rescale = float(total_rows) ** (-0.5)
    blocks = section_rows.reshape(3, sections, per_source, 1, width)
    outgoing = jnp.take(blocks, offsets, axis=1)
    incoming = lax.all_to_all(outgoing, "section", split_axis=1, concat_axis=3, tiled=True)
    target = incoming.reshape(3, seq_dev, width).astype(jnp.float32)
    whole_proj = lax.all_gather(proj, "section", axis=0, tiled=True)
    flat_student = student_rows.reshape(3 * seq_dev, student_width)
    student_blocks = flat_student.T.reshape(sections, student_width // sections, 3 * seq_dev)
    pred = jnp.dot(flat_student, whole_proj, preferred_element_type=jnp.float32).reshape(
        3, seq_dev, width
    )
    squares = jnp.sum(target * target, axis=-1)
    scale = lax.psum(squares, "tensor") / (width * tensors) + 1e-06
    diff = gains[:, None, :] * pred - target
    ratio = diff / scale[:, :, None]
    steer = (gains[:, None, :] * ratio).astype(jnp.bfloat16)
    flat_steer = steer.reshape(3 * seq_dev, width)
    partial_student = lax.dot_general(
        flat_steer, whole_proj, (((1,), (1,)), ((), ())), preferred_element_type=jnp.float32
    )
    grad_student = lax.psum_scatter(
        partial_student.reshape(3, seq_dev, student_width).astype(jnp.bfloat16),
        "tensor",
        scatter_dimension=2,
        tiled=True,
    ).astype(jnp.float32)
    sums = jnp.concatenate(
        [jnp.sum(ratio * pred, axis=1), jnp.sum(diff * ratio, axis=(0, 1))[None]], axis=0
    )
    sums = lax.psum(sums, "section")
    grad_gains = sums[:3] * rescale
    loss = lax.psum(jnp.sum(sums[3]), "tensor") / (2.0 * total_rows * width * tensors)
    grad_proj = reduce_terms(student_blocks, flat_steer, sections, rescale)
    return (loss, grad_student, grad_proj, grad_gains)


def solution(mesh):
    return jax.shard_map(
        body,
        mesh=mesh,
        in_specs=(
            P(None, "section", "tensor"),
            P(None, "section", None),
            P("section", "tensor"),
            P(None, "tensor"),
            P(),
        ),
        out_specs=(P(), P(None, "section", "tensor"), P("section", "tensor"), P(None, "tensor")),
        check_vma=False,
    )
```

```python
import functools

import jax
import jax.numpy as jnp
from jax import lax
from jax.experimental import pallas as pl
from jax.experimental.pallas import tpu as pltpu
from jax.sharding import PartitionSpec as P

MESH = pl.DeviceIdType.MESH
SUBS = 2


def ring_place(index, n):
    chip, core = index // 2, index % 2
    if n == 16:
        z, x = chip // 2, chip % 2
        place = z + x * (7 - 2 * z)
    else:
        a, b = chip // 4, chip % 4
        place = a * 4 + b + (a % 2) * (3 - 2 * b)
    return place * 2 + core


def ring_index(place, n):
    spot, core = place // 2, place % 2
    if n == 16:
        x = spot // 4
        z = spot + x * (7 - 2 * spot)
        chip = z * 2 + x
    else:
        a, b = spot // 4, spot % 4
        chip = a * 4 + b + (a % 2) * (3 - 2 * b)
    return chip * 2 + core


def reduce_kernel(n, rescale, st_ref, steer_ref, out_ref, slots, send_sem, recv_sem):
    tensor = lax.axis_index("tensor")
    me = ring_place(lax.axis_index("section"), n)
    right = ring_index((me + 1) % n, n)
    left = ring_index((me + n - 1) % n, n)
    towards = (right, left)
    wide = slots.shape[-1]

    barrier = pltpu.get_barrier_semaphore()
    for neighbour in towards:
        pl.semaphore_signal(barrier, inc=1, device_id=(neighbour, tensor), device_id_type=MESH)
    pl.semaphore_wait(barrier, 2)

    def columns(d, j):
        return pl.ds((d * SUBS + j) * wide, wide)

    def term(d, j, step):
        place = (me + 2 * n - 1 - step) % n if d == 0 else (me + 1 + step) % n
        return jnp.dot(
            st_ref[ring_index(place, n)],
            steer_ref[:, columns(d, j)],
            preferred_element_type=jnp.float32,
        )

    def copy(d, j, step):
        return pltpu.make_async_remote_copy(
            src_ref=slots.at[d, j, step],
            dst_ref=slots.at[d, j, step + 1],
            send_sem=send_sem.at[d, j, step],
            recv_sem=recv_sem.at[d, j, step],
            device_id=(towards[d], tensor),
            device_id_type=MESH,
        )

    for j in range(SUBS):
        for d in range(2):
            slots[d, j, 0] = term(d, j, 0).astype(jnp.bfloat16)
            copy(d, j, 0).start()

    def body(step, carry):
        for j in range(SUBS):
            for d in range(2):
                own = term(d, j, step)
                copy(d, j, step - 1).wait_recv()
                slots[d, j, step] = (slots[d, j, step].astype(jnp.float32) + own).astype(
                    jnp.bfloat16
                )
                copy(d, j, step).start()
        return carry

    lax.fori_loop(1, n - 1, body, 0)
    for j in range(SUBS):
        for d in range(2):
            own = term(d, j, n - 1)
            copy(d, j, n - 2).wait_recv()
            out_ref[:, columns(d, j)] = (
                slots[d, j, n - 1].astype(jnp.float32) + own
            ) * rescale

    def drain(step, carry):
        for j in range(SUBS):
            for d in range(2):
                copy(d, j, step).wait_send()
        return carry

    lax.fori_loop(0, n - 1, drain, 0)


def reduce_terms(student_blocks, steer, n, rescale):
    rows = student_blocks.shape[1]
    width = steer.shape[1]
    wide = width // (2 * SUBS)
    return pl.pallas_call(
        functools.partial(reduce_kernel, n, rescale),
        out_shape=jax.ShapeDtypeStruct((rows, width), jnp.float32),
        in_specs=[pl.BlockSpec(memory_space=pltpu.VMEM)] * 2,
        out_specs=pl.BlockSpec(memory_space=pltpu.VMEM),
        scratch_shapes=[
            pltpu.VMEM((2, SUBS, n, rows, wide), jnp.bfloat16),
            pltpu.SemaphoreType.DMA((2, SUBS, n)),
            pltpu.SemaphoreType.DMA((2, SUBS, n)),
        ],
        compiler_params=pltpu.CompilerParams(
            collective_id=0, has_side_effects=True, vmem_limit_bytes=52 * 1024 * 1024
        ),
        cost_estimate=pl.CostEstimate(
            flops=2 * n * rows * width * steer.shape[0],
            bytes_accessed=400_000_000,
            transcendentals=0,
        ),
        name="reduce_terms",
    )(student_blocks, steer)


def gather_kernel(n, proj_ref, student_ref, outgoing_ref, whole_ref, pred_ref, target_ref,
                  slots, send_sem, recv_sem, keep_sem, out_sem, in_sem, own_sem):
    tensor = lax.axis_index("tensor")
    index = lax.axis_index("section")
    me = ring_place(index, n)
    towards = (ring_index((me + 1) % n, n), ring_index((me + n - 1) % n, n))
    rows, wide = slots.shape[-2:]

    barrier = pltpu.get_barrier_semaphore()
    for s in range(1, n):
        pl.semaphore_signal(
            barrier, inc=1, device_id=((index + s) % n, tensor), device_id_type=MESH
        )
    pl.semaphore_wait(barrier, n - 1)

    def columns(d, j):
        return pl.ds((d * SUBS + j) * wide, wide)

    def owner(d, step):
        return ring_index((me + n - step) % n if d == 0 else (me + step) % n, n)

    def copy(d, j, step):
        return pltpu.make_async_remote_copy(
            src_ref=slots.at[d, j, step],
            dst_ref=slots.at[d, j, step + 1],
            send_sem=send_sem.at[d, j, step],
            recv_sem=recv_sem.at[d, j, step],
            device_id=(towards[d], tensor),
            device_id_type=MESH,
        )

    def keep(d, j, step):
        place = pl.ds(pl.multiple_of(owner(d, step) * rows, 16), rows)
        return pltpu.make_async_copy(
            slots.at[d, j, step], whole_ref.at[place, columns(d, j)], keep_sem.at[d, j, step]
        )

    def teach(s):
        there = (index + s) % n
        return pltpu.make_async_remote_copy(
            src_ref=outgoing_ref.at[there],
            dst_ref=target_ref.at[index],
            send_sem=out_sem.at[s],
            recv_sem=in_sem.at[index],
            device_id=(there, tensor),
            device_id_type=MESH,
        )

    def taught(s):
        source = (index + n - s) % n
        return pltpu.make_async_remote_copy(
            src_ref=outgoing_ref.at[source],
            dst_ref=target_ref.at[source],
            send_sem=out_sem.at[s],
            recv_sem=in_sem.at[source],
            device_id=(source, tensor),
            device_id_type=MESH,
        )

    def product(d, j, step):
        return jnp.dot(
            student_ref[owner(d, step)], slots[d, j, step], preferred_element_type=jnp.float32
        )

    for j in range(SUBS):
        for d in range(2):
            slots[d, j, 0] = proj_ref[:, columns(d, j)]
            copy(d, j, 0).start()
    own = pltpu.make_async_copy(outgoing_ref.at[index], target_ref.at[index], own_sem)
    own.start()
    teach(1).start()
    for j in range(SUBS):
        for d in range(2):
            keep(d, j, 0).start()
            pred_ref[:, columns(d, j)] = product(d, j, 0)

    def body(step, carry):
        teach(step + 1).start()
        for j in range(SUBS):
            for d in range(2):
                copy(d, j, step - 1).wait_recv()
                copy(d, j, step).start()
                keep(d, j, step).start()
                pred_ref[:, columns(d, j)] += product(d, j, step)
        return carry

    lax.fori_loop(1, n - 1, body, 0)
    for j in range(SUBS):
        for d in range(2):
            copy(d, j, n - 2).wait_recv()
            keep(d, j, n - 1).start()
            pred_ref[:, columns(d, j)] += product(d, j, n - 1)

    own.wait()

    def drain(step, carry):
        for j in range(SUBS):
            for d in range(2):
                copy(d, j, step).wait_send()
                keep(d, j, step).wait()
        teach(step + 1).wait_send()
        taught(step + 1).wait_recv()
        return carry

    lax.fori_loop(0, n - 1, drain, 0)
    for j in range(SUBS):
        for d in range(2):
            keep(d, j, n - 1).wait()


def gather_project(proj, student_blocks, outgoing):
    n, tokens, rows = student_blocks.shape
    width = proj.shape[1]
    wide = width // (2 * SUBS)
    return pl.pallas_call(
        functools.partial(gather_kernel, n),
        out_shape=(
            jax.ShapeDtypeStruct((n * rows, width), jnp.bfloat16),
            jax.ShapeDtypeStruct((tokens, width), jnp.float32),
            jax.ShapeDtypeStruct(outgoing.shape, jnp.bfloat16),
        ),
        in_specs=[
            pl.BlockSpec(memory_space=pltpu.VMEM),
            pl.BlockSpec(memory_space=pltpu.VMEM),
            pl.BlockSpec(memory_space=pl.ANY),
        ],
        out_specs=(
            pl.BlockSpec(memory_space=pl.ANY),
            pl.BlockSpec(memory_space=pltpu.VMEM),
            pl.BlockSpec(memory_space=pl.ANY),
        ),
        scratch_shapes=[
            pltpu.VMEM((2, SUBS, n, rows, wide), jnp.bfloat16),
            pltpu.SemaphoreType.DMA((2, SUBS, n)),
            pltpu.SemaphoreType.DMA((2, SUBS, n)),
            pltpu.SemaphoreType.DMA((2, SUBS, n)),
            pltpu.SemaphoreType.DMA((n,)),
            pltpu.SemaphoreType.DMA((n,)),
            pltpu.SemaphoreType.DMA,
        ],
        compiler_params=pltpu.CompilerParams(
            collective_id=1, has_side_effects=True, vmem_limit_bytes=52 * 1024 * 1024
        ),
        cost_estimate=pl.CostEstimate(
            flops=2 * n * rows * width * tokens, bytes_accessed=500_000_000, transcendentals=0
        ),
        name="gather_project",
    )(proj, student_blocks, outgoing)


def body(section_rows, student_rows, proj, gains, offsets):
    sections = lax.axis_size("section")
    tensors = lax.axis_size("tensor")
    seq_dev = student_rows.shape[1]
    width = section_rows.shape[2]
    student_width = student_rows.shape[2]
    per_source = seq_dev // sections
    total_rows = 3 * seq_dev * sections
    rescale = float(total_rows) ** (-0.5)
    parts = sections // 8
    part = width // parts
    per_rank = 3 * per_source
    blocks = section_rows.reshape(3, sections, per_source, width)
    outgoing = jnp.take(blocks, offsets, axis=1).transpose(1, 0, 2, 3)
    outgoing = outgoing.reshape(sections, per_rank, width)
    outgoing = jnp.concatenate(
        [outgoing[:, :, c * part : (c + 1) * part] for c in range(parts)], axis=1
    )
    ordered = student_rows.reshape(3, per_source, sections, student_width).transpose(2, 0, 1, 3)
    flat_student = ordered.reshape(3 * seq_dev, student_width)
    section_depth = student_width // sections
    student_blocks = flat_student.T.reshape(sections, section_depth, 3 * seq_dev)
    student_left = student_blocks.transpose(0, 2, 1)
    whole_proj, pred, incoming = gather_project(proj, student_left, outgoing)
    shape = (sections, 3, per_source, width)
    pred = pred.reshape(shape)
    target = jnp.concatenate(
        [incoming[:, c * per_rank : (c + 1) * per_rank] for c in range(parts)], axis=2
    )
    target = target.reshape(shape).astype(jnp.float32)
    squares = jnp.sum(target * target, axis=-1)
    scale = lax.psum(squares, "tensor") / (width * tensors) + 1e-06
    gain = gains[None, :, None, :]
    diff = gain * pred - target
    ratio = diff / scale[..., None]
    steer = (gain * ratio).astype(jnp.bfloat16)
    flat_steer = steer.reshape(3 * seq_dev, width)
    partial_student = lax.dot_general(
        flat_steer, whole_proj, (((1,), (1,)), ((), ())), preferred_element_type=jnp.float32
    )
    grad_student = lax.psum_scatter(
        partial_student.astype(jnp.bfloat16), "tensor", scatter_dimension=1, tiled=True
    )
    grad_student = grad_student.reshape(sections, 3, per_source, student_width // tensors)
    grad_student = grad_student.transpose(1, 2, 0, 3).reshape(3, seq_dev, -1).astype(jnp.float32)
    sums = jnp.concatenate(
        [jnp.sum(ratio * pred, axis=(0, 2)), jnp.sum(diff * ratio, axis=(0, 1, 2))[None]], axis=0
    )
    sums = lax.psum(sums, "section")
    grad_gains = sums[:3] * rescale
    loss = lax.psum(jnp.sum(sums[3]), "tensor") / (2.0 * total_rows * width * tensors)
    grad_proj = reduce_terms(student_blocks, flat_steer, sections, rescale)
    return (loss, grad_student, grad_proj, grad_gains)


def solution(mesh):
    return jax.shard_map(
        body,
        mesh=mesh,
        in_specs=(
            P(None, "section", "tensor"),
            P(None, "section", None),
            P("section", "tensor"),
            P(None, "tensor"),
            P(),
        ),
        out_specs=(P(), P(None, "section", "tensor"), P("section", "tensor"), P(None, "tensor")),
        check_vma=False,
    )
```

```python
import functools

import jax
import jax.numpy as jnp
from jax import lax
from jax.experimental import pallas as pl
from jax.experimental.pallas import tpu as pltpu
from jax.sharding import PartitionSpec as P

MESH = pl.DeviceIdType.MESH
SUBS = 4


def ring_place(index, n):
    chip, core = index // 2, index % 2
    if n == 16:
        z, x = chip // 2, chip % 2
        place = z + x * (7 - 2 * z)
    else:
        a, b = chip // 4, chip % 4
        place = a * 4 + b + (a % 2) * (3 - 2 * b)
    return place * 2 + core


def ring_index(place, n):
    spot, core = place // 2, place % 2
    if n == 16:
        x = spot // 4
        z = spot + x * (7 - 2 * spot)
        chip = z * 2 + x
    else:
        a, b = spot // 4, spot % 4
        chip = a * 4 + b + (a % 2) * (3 - 2 * b)
    return chip * 2 + core


def reduce_kernel(n, rescale, st_ref, steer_ref, out_ref, slots, send_sem, recv_sem):
    tensor = lax.axis_index("tensor")
    me = ring_place(lax.axis_index("section"), n)
    right = ring_index((me + 1) % n, n)
    left = ring_index((me + n - 1) % n, n)
    towards = (right, left)
    wide = slots.shape[-1]

    barrier = pltpu.get_barrier_semaphore()
    for neighbour in towards:
        pl.semaphore_signal(barrier, inc=1, device_id=(neighbour, tensor), device_id_type=MESH)
    pl.semaphore_wait(barrier, 2)

    def columns(d, j):
        return pl.ds((d * SUBS + j) * wide, wide)

    def term(d, j, step):
        place = (me + 2 * n - 1 - step) % n if d == 0 else (me + 1 + step) % n
        return jnp.dot(
            st_ref[ring_index(place, n)],
            steer_ref[:, columns(d, j)],
            preferred_element_type=jnp.float32,
        )

    def copy(d, j, step):
        return pltpu.make_async_remote_copy(
            src_ref=slots.at[d, j, step],
            dst_ref=slots.at[d, j, step + 1],
            send_sem=send_sem.at[d, j, step],
            recv_sem=recv_sem.at[d, j, step],
            device_id=(towards[d], tensor),
            device_id_type=MESH,
        )

    for j in range(SUBS):
        for d in range(2):
            slots[d, j, 0] = term(d, j, 0).astype(jnp.bfloat16)
            copy(d, j, 0).start()

    def body(step, carry):
        for j in range(SUBS):
            for d in range(2):
                own = term(d, j, step)
                copy(d, j, step - 1).wait_recv()
                slots[d, j, step] = (slots[d, j, step].astype(jnp.float32) + own).astype(
                    jnp.bfloat16
                )
                copy(d, j, step).start()
        return carry

    lax.fori_loop(1, n - 1, body, 0)
    for j in range(SUBS):
        for d in range(2):
            own = term(d, j, n - 1)
            copy(d, j, n - 2).wait_recv()
            out_ref[:, columns(d, j)] = (
                slots[d, j, n - 1].astype(jnp.float32) + own
            ) * rescale

    def drain(step, carry):
        for j in range(SUBS):
            for d in range(2):
                copy(d, j, step).wait_send()
        return carry

    lax.fori_loop(0, n - 1, drain, 0)


def reduce_terms(student_blocks, steer, n, rescale):
    rows = student_blocks.shape[1]
    width = steer.shape[1]
    wide = width // (2 * SUBS)
    return pl.pallas_call(
        functools.partial(reduce_kernel, n, rescale),
        out_shape=jax.ShapeDtypeStruct((rows, width), jnp.float32),
        in_specs=[pl.BlockSpec(memory_space=pltpu.VMEM)] * 2,
        out_specs=pl.BlockSpec(memory_space=pltpu.VMEM),
        scratch_shapes=[
            pltpu.VMEM((2, SUBS, n, rows, wide), jnp.bfloat16),
            pltpu.SemaphoreType.DMA((2, SUBS, n)),
            pltpu.SemaphoreType.DMA((2, SUBS, n)),
        ],
        compiler_params=pltpu.CompilerParams(
            collective_id=0, has_side_effects=True, vmem_limit_bytes=52 * 1024 * 1024
        ),
        cost_estimate=pl.CostEstimate(
            flops=2 * n * rows * width * steer.shape[0],
            bytes_accessed=400_000_000,
            transcendentals=0,
        ),
        name="reduce_terms",
    )(student_blocks, steer)


def body(section_rows, student_rows, proj, gains, offsets):
    sections = lax.axis_size("section")
    tensors = lax.axis_size("tensor")
    seq_dev = student_rows.shape[1]
    width = section_rows.shape[2]
    student_width = student_rows.shape[2]
    per_source = seq_dev // sections
    total_rows = 3 * seq_dev * sections
    rescale = float(total_rows) ** (-0.5)
    blocks = section_rows.reshape(3, sections, per_source, 1, width)
    outgoing = jnp.take(blocks, offsets, axis=1)
    incoming = lax.all_to_all(outgoing, "section", split_axis=1, concat_axis=3, tiled=True)
    target = incoming.reshape(3, seq_dev, width).astype(jnp.float32)
    whole_proj = lax.all_gather(proj, "section", axis=0, tiled=True)
    flat_student = student_rows.reshape(3 * seq_dev, student_width)
    student_blocks = flat_student.T.reshape(sections, student_width // sections, 3 * seq_dev)
    whole_proj, student_blocks = lax.optimization_barrier((whole_proj, student_blocks))
    pred = jnp.dot(flat_student, whole_proj, preferred_element_type=jnp.float32).reshape(
        3, seq_dev, width
    )
    squares = jnp.sum(target * target, axis=-1)
    scale = lax.psum(squares, "tensor") / (width * tensors) + 1e-06
    diff = gains[:, None, :] * pred - target
    ratio = diff / scale[:, :, None]
    steer = (gains[:, None, :] * ratio).astype(jnp.bfloat16)
    flat_steer = steer.reshape(3 * seq_dev, width)
    partial_student = lax.dot_general(
        flat_steer, whole_proj, (((1,), (1,)), ((), ())), preferred_element_type=jnp.float32
    )
    grad_student = lax.psum_scatter(
        partial_student.reshape(3, seq_dev, student_width).astype(jnp.bfloat16),
        "tensor",
        scatter_dimension=2,
        tiled=True,
    ).astype(jnp.float32)
    sums = jnp.concatenate(
        [jnp.sum(ratio * pred, axis=1), jnp.sum(diff * ratio, axis=(0, 1))[None]], axis=0
    )
    sums = lax.psum(sums, "section")
    grad_gains = sums[:3] * rescale
    loss = lax.psum(jnp.sum(sums[3]), "tensor") / (2.0 * total_rows * width * tensors)
    grad_proj = reduce_terms(student_blocks, flat_steer, sections, rescale)
    return (loss, grad_student, grad_proj, grad_gains)


def solution(mesh):
    return jax.shard_map(
        body,
        mesh=mesh,
        in_specs=(
            P(None, "section", "tensor"),
            P(None, "section", None),
            P("section", "tensor"),
            P(None, "tensor"),
            P(),
        ),
        out_specs=(P(), P(None, "section", "tensor"), P("section", "tensor"), P(None, "tensor")),
        check_vma=False,
    )
```

```python
import functools

import jax
import jax.numpy as jnp
from jax import lax
from jax.experimental import pallas as pl
from jax.experimental.pallas import tpu as pltpu
from jax.sharding import PartitionSpec as P

MESH = pl.DeviceIdType.MESH
SUBS = 2


def ring_place(index, n):
    chip, core = index // 2, index % 2
    if n == 16:
        z, x = chip // 2, chip % 2
        place = z + x * (7 - 2 * z)
    else:
        a, b = chip // 4, chip % 4
        place = a * 4 + b + (a % 2) * (3 - 2 * b)
    return place * 2 + core


def ring_index(place, n):
    spot, core = place // 2, place % 2
    if n == 16:
        x = spot // 4
        z = spot + x * (7 - 2 * spot)
        chip = z * 2 + x
    else:
        a, b = spot // 4, spot % 4
        chip = a * 4 + b + (a % 2) * (3 - 2 * b)
    return chip * 2 + core


def reduce_kernel(n, rescale, st_ref, steer_ref, out_ref, slots, send_sem, recv_sem):
    tensor = lax.axis_index("tensor")
    me = ring_place(lax.axis_index("section"), n)
    right = ring_index((me + 1) % n, n)
    left = ring_index((me + n - 1) % n, n)
    towards = (right, left)
    wide = slots.shape[-1]

    barrier = pltpu.get_barrier_semaphore()
    for neighbour in towards:
        pl.semaphore_signal(barrier, inc=1, device_id=(neighbour, tensor), device_id_type=MESH)
    pl.semaphore_wait(barrier, 2)

    def columns(d, j):
        return pl.ds((d * SUBS + j) * wide, wide)

    def term(d, j, step):
        place = (me + 2 * n - 1 - step) % n if d == 0 else (me + 1 + step) % n
        return jnp.dot(
            st_ref[ring_index(place, n)],
            steer_ref[:, columns(d, j)],
            preferred_element_type=jnp.float32,
        )

    def copy(d, j, step):
        return pltpu.make_async_remote_copy(
            src_ref=slots.at[d, j, step],
            dst_ref=slots.at[d, j, step + 1],
            send_sem=send_sem.at[d, j, step],
            recv_sem=recv_sem.at[d, j, step],
            device_id=(towards[d], tensor),
            device_id_type=MESH,
        )

    for j in range(SUBS):
        for d in range(2):
            slots[d, j, 0] = term(d, j, 0).astype(jnp.bfloat16)
            copy(d, j, 0).start()

    def body(step, carry):
        for j in range(SUBS):
            for d in range(2):
                own = term(d, j, step)
                copy(d, j, step - 1).wait_recv()
                slots[d, j, step] = (slots[d, j, step].astype(jnp.float32) + own).astype(
                    jnp.bfloat16
                )
                copy(d, j, step).start()
        return carry

    lax.fori_loop(1, n - 1, body, 0)
    for j in range(SUBS):
        for d in range(2):
            own = term(d, j, n - 1)
            copy(d, j, n - 2).wait_recv()
            out_ref[:, columns(d, j)] = (
                slots[d, j, n - 1].astype(jnp.float32) + own
            ) * rescale

    def drain(step, carry):
        for j in range(SUBS):
            for d in range(2):
                copy(d, j, step).wait_send()
        return carry

    lax.fori_loop(0, n - 1, drain, 0)


def reduce_terms(student_blocks, steer, n, rescale):
    rows = student_blocks.shape[1]
    width = steer.shape[1]
    wide = width // (2 * SUBS)
    return pl.pallas_call(
        functools.partial(reduce_kernel, n, rescale),
        out_shape=jax.ShapeDtypeStruct((rows, width), jnp.float32),
        in_specs=[pl.BlockSpec(memory_space=pltpu.VMEM)] * 2,
        out_specs=pl.BlockSpec(memory_space=pltpu.VMEM),
        scratch_shapes=[
            pltpu.VMEM((2, SUBS, n, rows, wide), jnp.bfloat16),
            pltpu.SemaphoreType.DMA((2, SUBS, n)),
            pltpu.SemaphoreType.DMA((2, SUBS, n)),
        ],
        compiler_params=pltpu.CompilerParams(
            collective_id=0, has_side_effects=True, vmem_limit_bytes=52 * 1024 * 1024
        ),
        cost_estimate=pl.CostEstimate(
            flops=2 * n * rows * width * steer.shape[0],
            bytes_accessed=400_000_000,
            transcendentals=0,
        ),
        name="reduce_terms",
    )(student_blocks, steer)


def body(section_rows, student_rows, proj, gains, offsets):
    sections = lax.axis_size("section")
    tensors = lax.axis_size("tensor")
    seq_dev = student_rows.shape[1]
    width = section_rows.shape[2]
    student_width = student_rows.shape[2]
    per_source = seq_dev // sections
    total_rows = 3 * seq_dev * sections
    rescale = float(total_rows) ** (-0.5)
    blocks = section_rows.reshape(3, sections, per_source, 1, width)
    outgoing = jnp.take(blocks, offsets, axis=1)
    flat_student = student_rows.reshape(3 * seq_dev, student_width)
    student_blocks = flat_student.T.reshape(sections, student_width // sections, 3 * seq_dev)
    outgoing, student_blocks = lax.optimization_barrier((outgoing, student_blocks))
    incoming = lax.all_to_all(outgoing, "section", split_axis=1, concat_axis=3, tiled=True)
    target = incoming.reshape(3, seq_dev, width).astype(jnp.float32)
    whole_proj = lax.all_gather(proj, "section", axis=0, tiled=True)
    pred = jnp.dot(flat_student, whole_proj, preferred_element_type=jnp.float32).reshape(
        3, seq_dev, width
    )
    squares = jnp.sum(target * target, axis=-1)
    scale = lax.psum(squares, "tensor") / (width * tensors) + 1e-06
    diff = gains[:, None, :] * pred - target
    ratio = diff / scale[:, :, None]
    steer = (gains[:, None, :] * ratio).astype(jnp.bfloat16)
    flat_steer = steer.reshape(3 * seq_dev, width)
    partial_student = lax.dot_general(
        flat_steer, whole_proj, (((1,), (1,)), ((), ())), preferred_element_type=jnp.float32
    )
    grad_student = lax.psum_scatter(
        partial_student.reshape(3, seq_dev, student_width).astype(jnp.bfloat16),
        "tensor",
        scatter_dimension=2,
        tiled=True,
    ).astype(jnp.float32)
    sums = jnp.concatenate(
        [jnp.sum(ratio * pred, axis=1), jnp.sum(diff * ratio, axis=(0, 1))[None]], axis=0
    )
    sums = lax.psum(sums, "section")
    grad_gains = sums[:3] * rescale
    loss = lax.psum(jnp.sum(sums[3]), "tensor") / (2.0 * total_rows * width * tensors)
    grad_proj = reduce_terms(student_blocks, flat_steer, sections, rescale)
    return (loss, grad_student, grad_proj, grad_gains)


def solution(mesh):
    return jax.shard_map(
        body,
        mesh=mesh,
        in_specs=(
            P(None, "section", "tensor"),
            P(None, "section", None),
            P("section", "tensor"),
            P(None, "tensor"),
            P(),
        ),
        out_specs=(P(), P(None, "section", "tensor"), P("section", "tensor"), P(None, "tensor")),
        check_vma=False,
    )
```
